32 devices in a mesh: layer: 8 (over y, x, core), feat: 4 (over z).
Axes of the slice: x: 2, y: 2, z: 4, core: 2. Of those that a mesh axis runs over, the one named last changes fastest.
Arguments:
- latents: bfloat16 [2048, 16384], P('layer', 'feat'), may hold values from 0.5 to 3
- block_lists: int32 [4, 16, 64], replicated, may hold values from 0 to 127, all different within a row
- decoders: bfloat16 [2, 16384, 32768], P(None, 'feat', 'layer'), may hold values from -0.03125 to 0.03125
- targets: bfloat16 [512, 32768], P('feat', 'layer'), may hold values from -6 to 6
Outputs:
- errors: bfloat16 [512, 32768], P('feat', 'layer')
- latent_grad: float32 [2048, 16384], P('layer', 'feat')
The draws below stay inside these ranges and needn't reach their ends.
Inputs may be any that keep to these rules, and one draw needn't show every extreme that they name: `block_lists`: each row names 64 different latent blocks, and every block is named by some row.
All inputs are finite; a program needn't handle non-finite values.
Results may differ from the reference program's by a relative error of at most 0.006.
Values may be sent and summed in bfloat16 or wider, within the bound.
A program may use at most 192 MiB of HBM per device.

```python
import jax
import jax.numpy as jnp
from jax import lax

D = 8192
FEAT = 16384
BLOCK = 128
LAYERS = 4
SPAN = 2
TOK = 512
TROWS = 32
NBLK = 128
ACTIVE = 64
TBLK = 16


def shard_levels(key, extent, pieces, smallest, top_value):
    loudness = 1.0
    for dim, blocks in pieces:
        steps = jax.random.uniform(jax.random.fold_in(jax.random.fold_in(key, 6), dim), (blocks,), jnp.float32, smallest / len(pieces), top_value / len(pieces))
        loudness = loudness * jnp.repeat(jnp.exp(steps), extent[dim] // blocks).reshape((-1,) + (1,) * (len(extent) - 1 - dim))
    return loudness


def picks_of(key, rows, number_of, top, lift):
    ranking = jax.random.permutation(jax.random.fold_in(key, 1), number_of)
    pull = ranking
    for power in range(3):
        pull = pull * pull // number_of
    pull = pull * lift // number_of
    lots = jax.random.randint(jax.random.fold_in(key, 2), (rows, number_of), 0, 4096) + pull
    sure = jax.random.permutation(jax.random.fold_in(key, 3), rows)[jnp.arange(number_of) % rows]
    lots = jnp.where(jnp.arange(rows)[:, None] == sure[None, :], 1 << 14, lots)
    priority = lots * number_of + jnp.arange(number_of)
    return lax.top_k(priority.astype(jnp.int32), top)[1].astype(jnp.int32)


def scatter_about(own_key, extent, spread, bound, pieces=(), kind=jnp.bfloat16):
    entries = jax.random.normal(own_key, extent, jnp.float32) * spread
    if len(pieces) > 0:
        entries = shard_levels(own_key, extent, pieces, -0.22, 0.18) * entries
    return jnp.clip(entries, min=-bound, max=bound).astype(kind)


def setup_inputs(seed: int = 0) -> dict:
    key_of = jax.random.split(jax.random.key(seed), 5)
    return {
        "latents": jnp.clip(0.5 + 2.5 * jax.random.uniform(key_of[0], (LAYERS * TOK, FEAT), jnp.float32) ** shard_levels(key_of[0], (LAYERS * TOK, FEAT), ((0, 8), (1, 4)), -0.2, 0.2), 0.5, 3.0).astype(jnp.bfloat16),
        "block_lists": picks_of(key_of[1], LAYERS * TBLK, NBLK, ACTIVE, 8192).reshape((LAYERS, TBLK, ACTIVE)),
        "decoders": scatter_about(key_of[2], (SPAN, FEAT, LAYERS * D), (SPAN * FEAT) ** -0.5, 0.03125, ((1, 4), (2, 8))),
        "targets": scatter_about(key_of[3], (TOK, LAYERS * D), 1.0, 6.0, ((0, 4), (1, 8))),
    }


def build_mask(block_lists):
    blocks = jnp.arange(NBLK, dtype=jnp.int32)
    hit = jnp.any(block_lists[:, :, :, None] == blocks[None, None, None, :], axis=2)
    hit = jnp.repeat(hit, TROWS, axis=1)
    return jnp.repeat(hit, BLOCK, axis=2)


def reference(latents, block_lists, decoders, targets):
    mask = build_mask(block_lists)
    values = latents.reshape(LAYERS, TOK, FEAT)
    active = jnp.where(mask, values, jnp.zeros_like(values))
    before = jnp.concatenate([jnp.zeros_like(active[:1]), active[:-1]], axis=0)
    wanted_all = targets.reshape(TOK, LAYERS, D)

    def one_layer(items):
        layer_id, own, prior = items
        weights = lax.dynamic_slice_in_dim(decoders, layer_id * D, D, 2)
        wanted = lax.dynamic_index_in_dim(wanted_all, layer_id, 1, keepdims=False)
        recon = jnp.dot(own, weights[0], preferred_element_type=jnp.float32)
        recon = recon + jnp.dot(prior, weights[1], preferred_element_type=jnp.float32)
        error = (recon - wanted.astype(jnp.float32)).astype(jnp.bfloat16)
        part_own = jnp.dot(error, weights[0].T, preferred_element_type=jnp.float32)
        part_prior = jnp.dot(error, weights[1].T, preferred_element_type=jnp.float32)
        return error, part_own, part_prior

    layer_ids = jnp.arange(LAYERS, dtype=jnp.int32)
    errors, part_own, part_prior = lax.map(one_layer, (layer_ids, active, before))
    errors_out = jnp.transpose(errors, (1, 0, 2)).reshape(TOK, LAYERS * D)
    later = jnp.concatenate([part_prior[1:], jnp.zeros_like(part_prior[:1])], axis=0)
    latent_grad = jnp.where(mask, part_own + later, jnp.zeros_like(part_own))
    return errors_out, latent_grad.reshape(LAYERS * TOK, FEAT)
```

```python
import jax
import jax.numpy as jnp
from jax import lax
from jax.sharding import PartitionSpec as P

D = 8192
BLOCK = 128
CHUNKS = 4
PARTS = 2


def swapped(value, axis, bit):
    mask = 2**bit
    pairs = [(source, source ^ mask) for source in range(lax.axis_size(axis))]
    return lax.ppermute(value, axis, pairs)


def passed_along(value, axis, steps):
    count = lax.axis_size(axis)
    first, last = (max(0, -steps), min(count, count - steps))
    return lax.ppermute(value, axis, [(source, source + steps) for source in range(first, last)])


def doubled(held_rows, partner_rows, upper_half):
    return jnp.where(
        upper_half,
        jnp.concatenate([partner_rows, held_rows], 0),
        jnp.concatenate([held_rows, partner_rows], 0),
    )


def pick_half(block, upper_half, axis):
    half_rows = block.shape[axis] // 2
    lower = lax.slice_in_dim(block, 0, half_rows, axis=axis)
    higher = lax.slice_in_dim(block, half_rows, 2 * half_rows, axis=axis)
    return (jnp.where(upper_half, higher, lower), jnp.where(upper_half, lower, higher))


def local(latents, block_lists, decoders, targets):
    layer_pos = lax.axis_index("layer")
    feat_pos = lax.axis_index("feat")
    width_cols = decoders.shape[2]
    groups = D // width_cols
    width_bits = groups.bit_length() - 1
    layer_id = layer_pos // groups
    member = layer_pos % groups
    quarter, feat_cols = latents.shape
    total_rows = quarter * groups
    block_rows = total_rows // block_lists.shape[1]
    blocks_here = feat_cols // BLOCK
    lists = lax.dynamic_index_in_dim(block_lists, layer_id, 0, keepdims=False)
    wanted = feat_pos * blocks_here + jnp.arange(blocks_here, dtype=jnp.int32)
    hit = jnp.any(lists[:, :, None] == wanted[None, None, :], axis=1)
    row_hit = jnp.repeat(hit, block_rows, axis=0)
    row_hit = lax.dynamic_slice_in_dim(row_hit, member * quarter, quarter, 0)
    tile_mask = jnp.repeat(row_hit, BLOCK, axis=1)
    own_tile = jnp.where(tile_mask, latents, jnp.zeros_like(latents))
    own_all = own_tile
    for bit_pos in range(width_bits):
        upper_half = member // (1 << bit_pos) % 2 == 1
        partner_rows = swapped(own_all, "layer", bit_pos)
        own_all = doubled(own_all, partner_rows, upper_half)
    prior_all = passed_along(own_all, "layer", groups)
    summed = jnp.dot(own_all, decoders[0], preferred_element_type=jnp.float32)
    recon_rows = lax.psum_scatter(
        summed + jnp.dot(prior_all, decoders[1], preferred_element_type=jnp.float32),
        "feat",
        scatter_dimension=0,
        tiled=True,
    )
    errors_here = (recon_rows - targets.astype(jnp.float32)).astype(jnp.bfloat16)
    grad_terms = jnp.einsum(
        "tc,kfc->ktf",
        lax.all_gather(errors_here, "feat", axis=0, tiled=True),
        decoders,
        preferred_element_type=jnp.float32,
    )
    grad_pair = grad_terms
    for bit_pos in reversed(range(width_bits)):
        upper_half = member // (1 << bit_pos) % 2 == 1
        kept_part, sent_part = pick_half(grad_pair, upper_half, 1)
        grad_pair = kept_part + swapped(sent_part.astype(jnp.bfloat16), "layer", bit_pos).astype(
            sent_part.dtype
        )
    from_next = passed_along(grad_pair[1].astype(jnp.bfloat16), "layer", -groups).astype(
        jnp.float32
    )
    combined = grad_pair[0] + from_next
    latent_grad = jnp.where(tile_mask, combined, jnp.zeros_like(combined))
    return (errors_here, latent_grad)


def feat_moved(value, pairs):
    return lax.ppermute(value, "feat", pairs)


def chain_local(latents, block_lists, decoders, targets):
    layer_pos = lax.axis_index("layer")
    feat_pos = lax.axis_index("feat")
    width_cols = decoders.shape[2]
    layer_id = layer_pos // 2
    member = layer_pos % 2
    held_rows, feat_cols = latents.shape
    half_rows = held_rows // 2
    block_rows = 2 * held_rows // block_lists.shape[1]
    blocks_here = feat_cols // BLOCK
    lists = lax.dynamic_index_in_dim(block_lists, layer_id, 0, keepdims=False)
    wanted = feat_pos * blocks_here + jnp.arange(blocks_here, dtype=jnp.int32)
    hit = jnp.any(lists[:, :, None] == wanted[None, None, :], axis=1)
    own_blocks = held_rows // block_rows
    hit = lax.dynamic_slice_in_dim(hit, member * own_blocks, own_blocks, 0)
    tile_mask = jnp.repeat(jnp.repeat(hit, block_rows, axis=0), BLOCK, axis=1)
    own_tile = jnp.where(tile_mask, latents, jnp.zeros_like(latents))
    inner = (feat_pos == 1) | (feat_pos == 2)
    targets_wide = targets.astype(jnp.float32)

    own_rows, prior_rows = [], []
    for half in range(2):
        mine = lax.slice_in_dim(own_tile, half * half_rows, (half + 1) * half_rows, axis=0)
        before = passed_along(mine, "layer", 2)
        own_rows.append(jnp.concatenate([mine, swapped(mine, "layer", 0)], 0))
        prior_rows.append(jnp.concatenate([before, swapped(before, "layer", 0)], 0))

    chunk_cols = width_cols // CHUNKS
    errors = []
    for half in range(2):
        wants = feat_pos % 2 == half
        first = wants & (feat_pos // 2 == member)
        second = wants & (feat_pos // 2 != member)
        pieces = []
        for chunk in range(CHUNKS):
            cols = slice(chunk * chunk_cols, (chunk + 1) * chunk_cols)
            partial = jnp.dot(own_rows[half], decoders[0, :, cols], preferred_element_type=jnp.float32)
            partial = partial + jnp.dot(
                prior_rows[half], decoders[1, :, cols], preferred_element_type=jnp.float32
            )
            goal = targets_wide[:, cols]
            none = jnp.zeros_like(goal)
            partial = partial - jnp.concatenate(
                [jnp.where(first, goal, none), jnp.where(second, goal, none)], 0
            )
            inward = feat_moved(partial.astype(jnp.bfloat16), [(0, 1), (3, 2)])
            partial = partial + inward.astype(jnp.float32)
            across = feat_moved(partial.astype(jnp.bfloat16), [(1, 2), (2, 1)])
            total = (partial + across.astype(jnp.float32)).astype(jnp.bfloat16)
            outward = feat_moved(total, [(1, 0), (2, 3)])
            pieces.append(jnp.where(inner, total, outward))
        errors.append(jnp.concatenate(pieces, 1))

    grads = []
    part_feats = feat_cols // PARTS
    for half in range(2):
        parts = []
        for part in range(PARTS):
            feats = slice(part * part_feats, (part + 1) * part_feats)
            sums = []
            for span in (1, 0):
                term = lax.dot_general(
                    errors[half],
                    decoders[span, feats],
                    (((1,), (1,)), ((), ())),
                    preferred_element_type=jnp.float32,
                )
                given = swapped(term[half_rows:].astype(jnp.bfloat16), "layer", 0)
                sums.append(term[:half_rows] + given.astype(jnp.float32))
            later = passed_along(sums[0].astype(jnp.bfloat16), "layer", -2)
            parts.append(sums[1] + later.astype(jnp.float32))
        grads.append(jnp.concatenate(parts, 1))
    combined = jnp.concatenate(grads, 0)
    latent_grad = jnp.where(tile_mask, combined, jnp.zeros_like(combined))

    by_half = jnp.where(feat_pos % 2 == 0, errors[0], errors[1])
    errors_here = jnp.where(
        feat_pos // 2 == member, by_half[:half_rows], by_half[half_rows:]
    )
    return (errors_here, latent_grad)


def solution(mesh):
    placed = (P("layer", "feat"), P(), P(None, "feat", "layer"), P("feat", "layer"))
    on_line = mesh.shape["feat"] == 4 and mesh.shape["layer"] == 8
    return jax.shard_map(
        chain_local if on_line else local,
        mesh=mesh,
        in_specs=placed,
        out_specs=(P("feat", "layer"), P("layer", "feat")),
        check_vma=False,
    )
```

```python
import jax
import jax.numpy as jnp
from jax import lax
from jax.sharding import PartitionSpec as P

D = 8192
BLOCK = 128
CHUNKS = 8
PARTS = 4


def swapped(value, axis, bit):
    mask = 2**bit
    pairs = [(source, source ^ mask) for source in range(lax.axis_size(axis))]
    return lax.ppermute(value, axis, pairs)


def passed_along(value, axis, steps):
    count = lax.axis_size(axis)
    first, last = (max(0, -steps), min(count, count - steps))
    return lax.ppermute(value, axis, [(source, source + steps) for source in range(first, last)])


def doubled(held_rows, partner_rows, upper_half):
    return jnp.where(
        upper_half,
        jnp.concatenate([partner_rows, held_rows], 0),
        jnp.concatenate([held_rows, partner_rows], 0),
    )


def pick_half(block, upper_half, axis):
    half_rows = block.shape[axis] // 2
    lower = lax.slice_in_dim(block, 0, half_rows, axis=axis)
    higher = lax.slice_in_dim(block, half_rows, 2 * half_rows, axis=axis)
    return (jnp.where(upper_half, higher, lower), jnp.where(upper_half, lower, higher))


def local(latents, block_lists, decoders, targets):
    layer_pos = lax.axis_index("layer")
    feat_pos = lax.axis_index("feat")
    width_cols = decoders.shape[2]
    groups = D // width_cols
    width_bits = groups.bit_length() - 1
    layer_id = layer_pos // groups
    member = layer_pos % groups
    quarter, feat_cols = latents.shape
    total_rows = quarter * groups
    block_rows = total_rows // block_lists.shape[1]
    blocks_here = feat_cols // BLOCK
    lists = lax.dynamic_index_in_dim(block_lists, layer_id, 0, keepdims=False)
    wanted = feat_pos * blocks_here + jnp.arange(blocks_here, dtype=jnp.int32)
    hit = jnp.any(lists[:, :, None] == wanted[None, None, :], axis=1)
    row_hit = jnp.repeat(hit, block_rows, axis=0)
    row_hit = lax.dynamic_slice_in_dim(row_hit, member * quarter, quarter, 0)
    tile_mask = jnp.repeat(row_hit, BLOCK, axis=1)
    own_tile = jnp.where(tile_mask, latents, jnp.zeros_like(latents))
    own_all = own_tile
    for bit_pos in range(width_bits):
        upper_half = member // (1 << bit_pos) % 2 == 1
        partner_rows = swapped(own_all, "layer", bit_pos)
        own_all = doubled(own_all, partner_rows, upper_half)
    prior_all = passed_along(own_all, "layer", groups)
    summed = jnp.dot(own_all, decoders[0], preferred_element_type=jnp.float32)
    recon_rows = lax.psum_scatter(
        summed + jnp.dot(prior_all, decoders[1], preferred_element_type=jnp.float32),
        "feat",
        scatter_dimension=0,
        tiled=True,
    )
    errors_here = (recon_rows - targets.astype(jnp.float32)).astype(jnp.bfloat16)
    grad_terms = jnp.einsum(
        "tc,kfc->ktf",
        lax.all_gather(errors_here, "feat", axis=0, tiled=True),
        decoders,
        preferred_element_type=jnp.float32,
    )
    grad_pair = grad_terms
    for bit_pos in reversed(range(width_bits)):
        upper_half = member // (1 << bit_pos) % 2 == 1
        kept_part, sent_part = pick_half(grad_pair, upper_half, 1)
        grad_pair = kept_part + swapped(sent_part.astype(jnp.bfloat16), "layer", bit_pos).astype(
            sent_part.dtype
        )
    from_next = passed_along(grad_pair[1].astype(jnp.bfloat16), "layer", -groups).astype(
        jnp.float32
    )
    combined = grad_pair[0] + from_next
    latent_grad = jnp.where(tile_mask, combined, jnp.zeros_like(combined))
    return (errors_here, latent_grad)


def tied(*values):
    return lax.optimization_barrier(values)


def chain_local(latents, block_lists, decoders, targets):
    layer_pos = lax.axis_index("layer")
    feat_pos = lax.axis_index("feat")
    width_cols = decoders.shape[2]
    layer_id = layer_pos // 2
    member = layer_pos % 2
    held_rows, feat_cols = latents.shape
    half_rows = held_rows // 2
    tok_blocks = block_lists.shape[1]
    block_rows = 2 * held_rows // tok_blocks
    blocks_here = feat_cols // BLOCK

    raw_before = [
        passed_along(latents[half * half_rows : (half + 1) * half_rows], "layer", 2)
        for half in range(2)
    ]
    raw_partner = swapped(latents, "layer", 0)

    wanted = feat_pos * blocks_here + jnp.arange(blocks_here, dtype=jnp.int32)

    def masked(rows, layer, owner, start):
        lists = lax.dynamic_index_in_dim(block_lists, layer, 0, keepdims=False)
        hit = jnp.any(lists[:, :, None] == wanted[None, None, :], axis=1)
        count = rows.shape[0] // block_rows
        first = owner * (tok_blocks // 2) + start // block_rows
        hit = lax.dynamic_slice_in_dim(hit, first, count, 0)
        tile_mask = jnp.repeat(jnp.repeat(hit, block_rows, axis=0), BLOCK, axis=1)
        return jnp.where(tile_mask, rows, jnp.zeros_like(rows))

    own_all = jnp.concatenate(
        [masked(latents, layer_id, member, 0), masked(raw_partner, layer_id, 1 - member, 0)], 0
    )
    (own_all,) = tied(own_all)

    goal_place = 2 * (feat_pos // 2 != member) + feat_pos % 2
    chunk_cols = width_cols // CHUNKS
    col_slices = [slice(c * chunk_cols, (c + 1) * chunk_cols) for c in range(CHUNKS)]
    own_parts = []
    for cols in col_slices:
        goal = targets[:, cols].astype(jnp.float32)
        none = jnp.zeros_like(goal)
        goal = jnp.concatenate([jnp.where(goal_place == p, goal, none) for p in range(4)], 0)
        own_parts.append(
            jnp.dot(own_all, decoders[0, :, cols], preferred_element_type=jnp.float32) - goal
        )

    raw_pieces = []
    for half, after in enumerate((CHUNKS - 2, CHUNKS)):
        values = tied(raw_before[half], *own_parts[:after])
        raw_pieces.append(values[0])
        own_parts[:after] = values[1:]
    prior_layer = jnp.maximum(layer_id - 1, 0)
    prior_all = jnp.concatenate(
        [
            masked(rows, prior_layer, owner, half * half_rows)
            for owner, held in (
                (member, raw_pieces),
                (1 - member, [swapped(piece, "layer", 0) for piece in raw_pieces]),
            )
            for half, rows in enumerate(held)
        ],
        0,
    )
    (prior_all,) = tied(prior_all)

    def narrow(value):
        return value.astype(jnp.bfloat16)

    early, late = range(CHUNKS // 2), range(CHUNKS // 2, CHUNKS)
    part_feats = feat_cols // PARTS
    feat_slices = [slice(p * part_feats, (p + 1) * part_feats) for p in range(PARTS)]
    jobs = [(span, p) for span in (1, 0) for p in range(PARTS)]

    def term(rows, span, part, chunks):
        cols = slice(chunks[0] * chunk_cols, (chunks[-1] + 1) * chunk_cols)
        return lax.dot_general(
            rows,
            decoders[span, feat_slices[part], cols],
            (((1,), (1,)), ((), ())),
            preferred_element_type=jnp.float32,
        )

    def recon(rows, chunk):
        return own_parts[chunk] + jnp.dot(
            rows, decoders[1, :, col_slices[chunk]], preferred_element_type=jnp.float32
        )

    inner = (feat_pos == 1) | (feat_pos == 2)
    routes = {"in": [(0, 1), (3, 2)], "across": [(1, 2), (2, 1)], "out": [(1, 0), (2, 3)]}
    partial, total, errors = [None] * CHUNKS, [None] * CHUNKS, [None] * CHUNKS
    partial[0] = recon(prior_all, 0)
    first_wave = len(early) + 2
    per_wave = len(jobs) // (CHUNKS + 2 - first_wave)
    early_errors, early_terms = None, {}
    for wave in range(CHUNKS + 2):
        sent = {"rows": prior_all}
        if wave < CHUNKS:
            sent["in"] = narrow(partial[wave])
        if 0 <= wave - 1 < CHUNKS:
            sent["across"] = narrow(partial[wave - 1])
        if 0 <= wave - 2 < CHUNKS:
            sent["out"] = total[wave - 2]
        if wave == first_wave:
            early_errors = jnp.concatenate([errors[c] for c in early], 1)
        if early_errors is not None:
            sent["early"] = early_errors
        held = dict(zip(sent, tied(*sent.values())))
        got = {name: lax.ppermute(held[name], "feat", routes[name]) for name in routes if name in held}
        if wave + 1 < CHUNKS:
            got["next"] = recon(held["rows"], wave + 1)
        if early_errors is not None:
            early_errors = held["early"]
            first_job = (wave - first_wave) * per_wave
            for job in jobs[first_job : first_job + per_wave]:
                got[job] = term(early_errors, *job, early)
        got = dict(zip(got, tied(*got.values())))
        if "next" in got:
            partial[wave + 1] = got["next"]
        if "in" in got:
            partial[wave] = partial[wave] + got["in"].astype(jnp.float32)
        if "across" in got:
            total[wave - 1] = narrow(partial[wave - 1] + got["across"].astype(jnp.float32))
        if "out" in got:
            errors[wave - 2] = jnp.where(inner, held["out"], got["out"])
        early_terms.update({job: got[job] for job in jobs if job in got})

    late_errors = jnp.concatenate([errors[c] for c in late], 1)
    held_terms, given, sums = [], [], []

    def finish(step):
        value = held_terms[step] + swapped(given[step], "layer", 0).astype(jnp.float32)
        sums.append(narrow(value) if jobs[step][0] == 1 else value)

    for step, job in enumerate(jobs):
        if step >= 2:
            finish(step - 2)
            late_errors, sums[-1], given[-1] = tied(late_errors, sums[-1], given[-1])
        elif step == 1:
            late_errors, given[-1] = tied(late_errors, given[-1])
        whole = early_terms[job] + term(late_errors, *job, late)
        held_terms.append(whole[:held_rows])
        given.append(narrow(whole[held_rows:]))
    finish(len(jobs) - 2)
    finish(len(jobs) - 1)
    later = [passed_along(value, "layer", -2) for value in sums[:PARTS]]
    pieces = [mine + more.astype(jnp.float32) for mine, more in zip(sums[PARTS:], later)]
    latent_grad = masked(jnp.concatenate(pieces, 1), layer_id, member, 0)

    error_rows = [jnp.concatenate(errors, 1)[p * half_rows : (p + 1) * half_rows] for p in range(4)]
    errors_here = error_rows[3]
    for p in range(3):
        errors_here = jnp.where(goal_place == p, error_rows[p], errors_here)
    return (errors_here, latent_grad)


def solution(mesh):
    placed = (P("layer", "feat"), P(), P(None, "feat", "layer"), P("feat", "layer"))
    on_line = mesh.shape["feat"] == 4 and mesh.shape["layer"] == 8
    return jax.shard_map(
        chain_local if on_line else local,
        mesh=mesh,
        in_specs=placed,
        out_specs=(P("feat", "layer"), P("layer", "feat")),
        check_vma=False,
    )
```

```python
import functools

import jax
import jax.numpy as jnp
from jax import lax
from jax.experimental import pallas as pl
from jax.experimental.pallas import tpu as pltpu
from jax.sharding import PartitionSpec as P

D = 8192
BLOCK = 128
CHUNKS = 32
PARTS = 4


def swapped(value, axis, bit):
    mask = 2**bit
    pairs = [(source, source ^ mask) for source in range(lax.axis_size(axis))]
    return lax.ppermute(value, axis, pairs)


def passed_along(value, axis, steps):
    count = lax.axis_size(axis)
    first, last = (max(0, -steps), min(count, count - steps))
    return lax.ppermute(value, axis, [(source, source + steps) for source in range(first, last)])


def doubled(held_rows, partner_rows, upper_half):
    return jnp.where(
        upper_half,
        jnp.concatenate([partner_rows, held_rows], 0),
        jnp.concatenate([held_rows, partner_rows], 0),
    )


def pick_half(block, upper_half, axis):
    half_rows = block.shape[axis] // 2
    lower = lax.slice_in_dim(block, 0, half_rows, axis=axis)
    higher = lax.slice_in_dim(block, half_rows, 2 * half_rows, axis=axis)
    return (jnp.where(upper_half, higher, lower), jnp.where(upper_half, lower, higher))


def local(latents, block_lists, decoders, targets):
    layer_pos = lax.axis_index("layer")
    feat_pos = lax.axis_index("feat")
    width_cols = decoders.shape[2]
    groups = D // width_cols
    width_bits = groups.bit_length() - 1
    layer_id = layer_pos // groups
    member = layer_pos % groups
    quarter, feat_cols = latents.shape
    total_rows = quarter * groups
    block_rows = total_rows // block_lists.shape[1]
    blocks_here = feat_cols // BLOCK
    lists = lax.dynamic_index_in_dim(block_lists, layer_id, 0, keepdims=False)
    wanted = feat_pos * blocks_here + jnp.arange(blocks_here, dtype=jnp.int32)
    hit = jnp.any(lists[:, :, None] == wanted[None, None, :], axis=1)
    row_hit = jnp.repeat(hit, block_rows, axis=0)
    row_hit = lax.dynamic_slice_in_dim(row_hit, member * quarter, quarter, 0)
    tile_mask = jnp.repeat(row_hit, BLOCK, axis=1)
    own_tile = jnp.where(tile_mask, latents, jnp.zeros_like(latents))
    own_all = own_tile
    for bit_pos in range(width_bits):
        upper_half = member // (1 << bit_pos) % 2 == 1
        partner_rows = swapped(own_all, "layer", bit_pos)
        own_all = doubled(own_all, partner_rows, upper_half)
    prior_all = passed_along(own_all, "layer", groups)
    summed = jnp.dot(own_all, decoders[0], preferred_element_type=jnp.float32)
    recon_rows = lax.psum_scatter(
        summed + jnp.dot(prior_all, decoders[1], preferred_element_type=jnp.float32),
        "feat",
        scatter_dimension=0,
        tiled=True,
    )
    errors_here = (recon_rows - targets.astype(jnp.float32)).astype(jnp.bfloat16)
    grad_terms = jnp.einsum(
        "tc,kfc->ktf",
        lax.all_gather(errors_here, "feat", axis=0, tiled=True),
        decoders,
        preferred_element_type=jnp.float32,
    )
    grad_pair = grad_terms
    for bit_pos in reversed(range(width_bits)):
        upper_half = member // (1 << bit_pos) % 2 == 1
        kept_part, sent_part = pick_half(grad_pair, upper_half, 1)
        grad_pair = kept_part + swapped(sent_part.astype(jnp.bfloat16), "layer", bit_pos).astype(
            sent_part.dtype
        )
    from_next = passed_along(grad_pair[1].astype(jnp.bfloat16), "layer", -groups).astype(
        jnp.float32
    )
    combined = grad_pair[0] + from_next
    latent_grad = jnp.where(tile_mask, combined, jnp.zeros_like(combined))
    return (errors_here, latent_grad)


def line_kernel(
    chunks, partial, errors, sent, got_in, got_across, in_out, in_in, over_out, over_in, back_out, back_in
):
    me = lax.axis_index("feat")
    partner = me + 1 - 2 * (me % 2)
    inner = (me == 1) | (me == 2)
    rows = partial.shape[0] // chunks

    def block(c):
        return pl.ds(pl.multiple_of(c * rows, rows), rows)

    def copy(c, source, target, out_sems, in_sems, owner):
        return pltpu.make_async_remote_copy(
            src_ref=source.at[block(c)],
            dst_ref=target.at[block(c)],
            send_sem=out_sems.at[c],
            recv_sem=in_sems.at[c],
            device_id={"feat": owner},
            device_id_type=pl.DeviceIdType.MESH,
        )

    def inward(c):
        return copy(c, sent, got_in, in_out, in_in, partner)

    def across(c):
        return copy(c, sent, got_across, over_out, over_in, 3 - me)

    def outward(c):
        return copy(c, errors, errors, back_out, back_in, partner)

    def each(first, last, body):
        def step(c, carry):
            body(c)
            return carry

        lax.fori_loop(first, last, step, 0)

    barrier = pltpu.get_barrier_semaphore()
    pl.semaphore_signal(
        barrier, inc=1, device_id={"feat": partner}, device_id_type=pl.DeviceIdType.MESH
    )

    @pl.when(inner)
    def _():
        pl.semaphore_signal(
            barrier, inc=1, device_id={"feat": 3 - me}, device_id_type=pl.DeviceIdType.MESH
        )
        pl.semaphore_wait(barrier, 2)

        def gather(c):
            inward(c).wait_recv()
            total = partial[block(c), :] + got_in[block(c), :].astype(jnp.float32)
            sent[block(c), :] = total.astype(jnp.bfloat16)
            across(c).start()

        def spread(c):
            across(c).wait_recv()
            total = sent[block(c), :].astype(jnp.float32) + got_across[block(c), :].astype(jnp.float32)
            errors[block(c), :] = total.astype(jnp.bfloat16)
            outward(c).start()

        def both(c):
            gather(c)
            spread(c - 1)

        gather(0)
        each(1, chunks, both)
        spread(chunks - 1)

        def drain(c):
            across(c).wait_send()
            outward(c).wait_send()

        each(0, chunks, drain)

    @pl.when(jnp.logical_not(inner))
    def _():
        pl.semaphore_wait(barrier, 1)

        def send(c):
            sent[block(c), :] = partial[block(c), :].astype(jnp.bfloat16)
            inward(c).start()

        def drain(c):
            inward(c).wait_send()
            outward(c).wait_recv()

        each(0, chunks, send)
        each(0, chunks, drain)


def summed_on_line(partial):
    shape = partial.shape
    return pl.pallas_call(
        functools.partial(line_kernel, CHUNKS),
        out_shape=jax.ShapeDtypeStruct(shape, jnp.bfloat16),
        in_specs=[pl.BlockSpec(memory_space=pltpu.VMEM)],
        out_specs=pl.BlockSpec(memory_space=pltpu.VMEM),
        scratch_shapes=[pltpu.VMEM(shape, jnp.bfloat16)] * 3
        + [pltpu.SemaphoreType.DMA((CHUNKS,))] * 6,
        compiler_params=pltpu.CompilerParams(
            collective_id=0, has_side_effects=True, vmem_limit_bytes=48 * 1024 * 1024
        ),
        cost_estimate=pl.CostEstimate(
            flops=4 * shape[0] * shape[1], bytes_accessed=6 * shape[0] * shape[1], transcendentals=0
        ),
    )(partial)


def tied(*values):
    return lax.optimization_barrier(values)


def chain_local(latents, block_lists, decoders, targets):
    layer_pos = lax.axis_index("layer")
    feat_pos = lax.axis_index("feat")
    width_cols = decoders.shape[2]
    layer_id = layer_pos // 2
    member = layer_pos % 2
    held_rows, feat_cols = latents.shape
    half_rows = held_rows // 2
    tok_blocks = block_lists.shape[1]
    block_rows = 2 * held_rows // tok_blocks
    blocks_here = feat_cols // BLOCK

    raw_before = passed_along(latents, "layer", 2)
    raw_partner = swapped(latents, "layer", 0)
    wanted = feat_pos * blocks_here + jnp.arange(blocks_here, dtype=jnp.int32)

    def mask_of(layer, owner):
        lists = lax.dynamic_index_in_dim(block_lists, layer, 0, keepdims=False)
        hit = jnp.any(lists[:, :, None] == wanted[None, None, :], axis=1)
        count = tok_blocks // 2
        hit = lax.dynamic_slice_in_dim(hit, owner * count, count, 0)
        return jnp.repeat(jnp.repeat(hit, block_rows, axis=0), BLOCK, axis=1)

    def masked(rows, mask):
        return jnp.where(mask, rows, jnp.zeros_like(rows))

    prior_layer = jnp.maximum(layer_id - 1, 0)
    own_mask = mask_of(layer_id, member)
    own_all = jnp.concatenate(
        [masked(latents, own_mask), masked(raw_partner, mask_of(layer_id, 1 - member))], 0
    )
    own_all, prior_mask, prior_mask_partner = tied(
        own_all, mask_of(prior_layer, member), mask_of(prior_layer, 1 - member)
    )

    goal_place = 2 * (feat_pos // 2 != member) + feat_pos % 2
    own_part = jnp.dot(own_all, decoders[0], preferred_element_type=jnp.float32)

    raw_prior, own_part = tied(raw_before, own_part)
    prior_all = jnp.concatenate(
        [
            masked(raw_prior, prior_mask),
            masked(swapped(raw_prior, "layer", 0), prior_mask_partner),
        ],
        0,
    )
    (prior_all,) = tied(prior_all)

    def narrow(value):
        return value.astype(jnp.bfloat16)

    goal = targets.astype(jnp.float32)
    none = jnp.zeros_like(goal)
    goal = jnp.concatenate([jnp.where(goal_place == p, goal, none) for p in range(4)], 0)
    partial = own_part + jnp.dot(prior_all, decoders[1], preferred_element_type=jnp.float32)
    errors = summed_on_line(partial - goal)

    jobs = [(span, p) for span in (1, 0) for p in range(PARTS)]
    held_terms, given, sums = [], [], []
    size = feat_cols // PARTS

    def finish(step):
        value = held_terms[step] + swapped(given[step], "layer", 0).astype(jnp.float32)
        sums.append(narrow(value) if jobs[step][0] == 1 else value)

    rows = errors
    for step, (span, part) in enumerate(jobs):
        if step >= 2:
            finish(step - 2)
            rows, sums[-1], given[-1] = tied(rows, sums[-1], given[-1])
        elif step == 1:
            rows, given[-1] = tied(rows, given[-1])
        term = lax.dot_general(
            rows,
            decoders[span, part * size : (part + 1) * size],
            (((1,), (1,)), ((), ())),
            preferred_element_type=jnp.float32,
        )
        held_terms.append(term[:held_rows])
        given.append(narrow(term[held_rows:]))
    finish(len(jobs) - 2)
    finish(len(jobs) - 1)
    later = [passed_along(value, "layer", -2) for value in sums[:PARTS]]
    pieces = [mine + more.astype(jnp.float32) for mine, more in zip(sums[PARTS:], later)]
    latent_grad = masked(jnp.concatenate(pieces, 1), own_mask)

    error_rows = [errors[p * half_rows : (p + 1) * half_rows] for p in range(4)]
    errors_here = error_rows[3]
    for p in range(3):
        errors_here = jnp.where(goal_place == p, error_rows[p], errors_here)
    return (errors_here, latent_grad)


def solution(mesh):
    placed = (P("layer", "feat"), P(), P(None, "feat", "layer"), P("feat", "layer"))
    on_line = mesh.shape["feat"] == 4 and mesh.shape["layer"] == 8
    return jax.shard_map(
        chain_local if on_line else local,
        mesh=mesh,
        in_specs=placed,
        out_specs=(P("feat", "layer"), P("layer", "feat")),
        check_vma=False,
    )
```

```python
import functools

import jax
import jax.numpy as jnp
from jax import lax
from jax.experimental import pallas as pl
from jax.experimental.pallas import tpu as pltpu
from jax.sharding import PartitionSpec as P

D = 8192
BLOCK = 128
CHUNKS = 32
PARTS = 4


def swapped(value, axis, bit):
    mask = 2**bit
    pairs = [(source, source ^ mask) for source in range(lax.axis_size(axis))]
    return lax.ppermute(value, axis, pairs)


def passed_along(value, axis, steps):
    count = lax.axis_size(axis)
    first, last = (max(0, -steps), min(count, count - steps))
    return lax.ppermute(value, axis, [(source, source + steps) for source in range(first, last)])


def doubled(held_rows, partner_rows, upper_half):
    return jnp.where(
        upper_half,
        jnp.concatenate([partner_rows, held_rows], 0),
        jnp.concatenate([held_rows, partner_rows], 0),
    )


def pick_half(block, upper_half, axis):
    half_rows = block.shape[axis] // 2
    lower = lax.slice_in_dim(block, 0, half_rows, axis=axis)
    higher = lax.slice_in_dim(block, half_rows, 2 * half_rows, axis=axis)
    return (jnp.where(upper_half, higher, lower), jnp.where(upper_half, lower, higher))


def local(latents, block_lists, decoders, targets):
    layer_pos = lax.axis_index("layer")
    feat_pos = lax.axis_index("feat")
    width_cols = decoders.shape[2]
    groups = D // width_cols
    width_bits = groups.bit_length() - 1
    layer_id = layer_pos // groups
    member = layer_pos % groups
    quarter, feat_cols = latents.shape
    total_rows = quarter * groups
    block_rows = total_rows // block_lists.shape[1]
    blocks_here = feat_cols // BLOCK
    lists = lax.dynamic_index_in_dim(block_lists, layer_id, 0, keepdims=False)
    wanted = feat_pos * blocks_here + jnp.arange(blocks_here, dtype=jnp.int32)
    hit = jnp.any(lists[:, :, None] == wanted[None, None, :], axis=1)
    row_hit = jnp.repeat(hit, block_rows, axis=0)
    row_hit = lax.dynamic_slice_in_dim(row_hit, member * quarter, quarter, 0)
    tile_mask = jnp.repeat(row_hit, BLOCK, axis=1)
    own_tile = jnp.where(tile_mask, latents, jnp.zeros_like(latents))
    own_all = own_tile
    for bit_pos in range(width_bits):
        upper_half = member // (1 << bit_pos) % 2 == 1
        partner_rows = swapped(own_all, "layer", bit_pos)
        own_all = doubled(own_all, partner_rows, upper_half)
    prior_all = passed_along(own_all, "layer", groups)
    summed = jnp.dot(own_all, decoders[0], preferred_element_type=jnp.float32)
    recon_rows = lax.psum_scatter(
        summed + jnp.dot(prior_all, decoders[1], preferred_element_type=jnp.float32),
        "feat",
        scatter_dimension=0,
        tiled=True,
    )
    errors_here = (recon_rows - targets.astype(jnp.float32)).astype(jnp.bfloat16)
    grad_terms = jnp.einsum(
        "tc,kfc->ktf",
        lax.all_gather(errors_here, "feat", axis=0, tiled=True),
        decoders,
        preferred_element_type=jnp.float32,
    )
    grad_pair = grad_terms
    for bit_pos in reversed(range(width_bits)):
        upper_half = member // (1 << bit_pos) % 2 == 1
        kept_part, sent_part = pick_half(grad_pair, upper_half, 1)
        grad_pair = kept_part + swapped(sent_part.astype(jnp.bfloat16), "layer", bit_pos).astype(
            sent_part.dtype
        )
    from_next = passed_along(grad_pair[1].astype(jnp.bfloat16), "layer", -groups).astype(
        jnp.float32
    )
    combined = grad_pair[0] + from_next
    latent_grad = jnp.where(tile_mask, combined, jnp.zeros_like(combined))
    return (errors_here, latent_grad)


def line_kernel(
    chunks, partial, errors, sent, got_in, got_across, in_out, in_in, over_out, over_in, back_out, back_in
):
    me = lax.axis_index("feat")
    partner = me + 1 - 2 * (me % 2)
    inner = (me == 1) | (me == 2)
    rows = partial.shape[0] // chunks

    def block(c):
        return pl.ds(pl.multiple_of(c * rows, rows), rows)

    def copy(c, source, target, out_sems, in_sems, owner):
        return pltpu.make_async_remote_copy(
            src_ref=source.at[block(c)],
            dst_ref=target.at[block(c)],
            send_sem=out_sems.at[c],
            recv_sem=in_sems.at[c],
            device_id={"feat": owner},
            device_id_type=pl.DeviceIdType.MESH,
        )

    def inward(c):
        return copy(c, sent, got_in, in_out, in_in, partner)

    def across(c):
        return copy(c, sent, got_across, over_out, over_in, 3 - me)

    def outward(c):
        return copy(c, errors, errors, back_out, back_in, partner)

    def each(first, last, body):
        def step(c, carry):
            body(c)
            return carry

        lax.fori_loop(first, last, step, 0)

    barrier = pltpu.get_barrier_semaphore()
    pl.semaphore_signal(
        barrier, inc=1, device_id={"feat": partner}, device_id_type=pl.DeviceIdType.MESH
    )

    @pl.when(inner)
    def _():
        pl.semaphore_signal(
            barrier, inc=1, device_id={"feat": 3 - me}, device_id_type=pl.DeviceIdType.MESH
        )
        pl.semaphore_wait(barrier, 2)

        def gather(c):
            inward(c).wait_recv()
            total = partial[block(c), :] + got_in[block(c), :].astype(jnp.float32)
            sent[block(c), :] = total.astype(jnp.bfloat16)
            across(c).start()

        def spread(c):
            across(c).wait_recv()
            total = sent[block(c), :].astype(jnp.float32) + got_across[block(c), :].astype(jnp.float32)
            errors[block(c), :] = total.astype(jnp.bfloat16)
            outward(c).start()

        def both(c):
            gather(c)
            spread(c - 1)

        gather(0)
        each(1, chunks, both)
        spread(chunks - 1)

        def drain(c):
            across(c).wait_send()
            outward(c).wait_send()

        each(0, chunks, drain)

    @pl.when(jnp.logical_not(inner))
    def _():
        pl.semaphore_wait(barrier, 1)

        def send(c):
            sent[block(c), :] = partial[block(c), :].astype(jnp.bfloat16)
            inward(c).start()

        def drain(c):
            inward(c).wait_send()
            outward(c).wait_recv()

        each(0, chunks, send)
        each(0, chunks, drain)


def summed_on_line(partial):
    shape = partial.shape
    return pl.pallas_call(
        functools.partial(line_kernel, CHUNKS),
        out_shape=jax.ShapeDtypeStruct(shape, jnp.bfloat16),
        in_specs=[pl.BlockSpec(memory_space=pltpu.VMEM)],
        out_specs=pl.BlockSpec(memory_space=pltpu.VMEM),
        scratch_shapes=[pltpu.VMEM(shape, jnp.bfloat16)] * 3
        + [pltpu.SemaphoreType.DMA((CHUNKS,))] * 6,
        compiler_params=pltpu.CompilerParams(
            collective_id=0, has_side_effects=True, vmem_limit_bytes=48 * 1024 * 1024
        ),
        cost_estimate=pl.CostEstimate(
            flops=4 * shape[0] * shape[1], bytes_accessed=6 * shape[0] * shape[1], transcendentals=0
        ),
    )(partial)


def tied(*values):
    return lax.optimization_barrier(values)


def chain_local(latents, block_lists, decoders, targets):
    layer_pos = lax.axis_index("layer")
    feat_pos = lax.axis_index("feat")
    width_cols = decoders.shape[2]
    layer_id = layer_pos // 2
    member = layer_pos % 2
    held_rows, feat_cols = latents.shape
    half_rows = held_rows // 2
    tok_blocks = block_lists.shape[1]
    block_rows = 2 * held_rows // tok_blocks
    blocks_here = feat_cols // BLOCK

    raw_before = passed_along(latents, "layer", 2)
    raw_partner = swapped(latents, "layer", 0)
    wanted = feat_pos * blocks_here + jnp.arange(blocks_here, dtype=jnp.int32)

    def mask_of(layer, owner):
        lists = lax.dynamic_index_in_dim(block_lists, layer, 0, keepdims=False)
        hit = jnp.any(lists[:, :, None] == wanted[None, None, :], axis=1)
        count = tok_blocks // 2
        hit = lax.dynamic_slice_in_dim(hit, owner * count, count, 0)
        return jnp.repeat(jnp.repeat(hit, block_rows, axis=0), BLOCK, axis=1)

    def masked(rows, mask):
        return jnp.where(mask, rows, jnp.zeros_like(rows))

    prior_layer = jnp.maximum(layer_id - 1, 0)
    own_mask = mask_of(layer_id, member)
    own_all = jnp.concatenate(
        [masked(latents, own_mask), masked(raw_partner, mask_of(layer_id, 1 - member))], 0
    )
    own_all, prior_mask, prior_mask_partner = tied(
        own_all, mask_of(prior_layer, member), mask_of(prior_layer, 1 - member)
    )

    goal_place = 2 * (feat_pos // 2 != member) + feat_pos % 2
    own_part = jnp.dot(own_all, decoders[0], preferred_element_type=jnp.float32)
    at_goal = jnp.arange(4)[:, None, None] == goal_place
    goal = jnp.where(at_goal, targets.astype(jnp.float32)[None], 0.0)
    own_part = own_part - goal.reshape(own_part.shape)

    raw_prior, own_part = tied(raw_before, own_part)
    prior_all = jnp.concatenate(
        [
            masked(raw_prior, prior_mask),
            masked(swapped(raw_prior, "layer", 0), prior_mask_partner),
        ],
        0,
    )
    (prior_all,) = tied(prior_all)

    def narrow(value):
        return value.astype(jnp.bfloat16)

    partial = own_part + jnp.dot(prior_all, decoders[1], preferred_element_type=jnp.float32)
    errors = summed_on_line(partial)

    jobs = [(span, p) for span in (1, 0) for p in range(PARTS)]
    held_terms, given, sums = [], [], []
    size = feat_cols // PARTS

    def finish(step):
        value = held_terms[step] + swapped(given[step], "layer", 0).astype(jnp.float32)
        sums.append(narrow(value) if jobs[step][0] == 1 else value)

    rows = errors
    for step, (span, part) in enumerate(jobs):
        if step >= 2:
            finish(step - 2)
            rows, sums[-1], given[-1] = tied(rows, sums[-1], given[-1])
        elif step == 1:
            rows, given[-1] = tied(rows, given[-1])
        term = lax.dot_general(
            rows,
            decoders[span, part * size : (part + 1) * size],
            (((1,), (1,)), ((), ())),
            preferred_element_type=jnp.float32,
        )
        held_terms.append(term[:held_rows])
        given.append(narrow(term[held_rows:]))
    finish(len(jobs) - 2)
    finish(len(jobs) - 1)
    later = [passed_along(value, "layer", -2) for value in sums[:PARTS]]
    pieces = [mine + more.astype(jnp.float32) for mine, more in zip(sums[PARTS:], later)]
    latent_grad = masked(jnp.concatenate(pieces, 1), own_mask)

    error_rows = [errors[p * half_rows : (p + 1) * half_rows] for p in range(4)]
    errors_here = error_rows[3]
    for p in range(3):
        errors_here = jnp.where(goal_place == p, error_rows[p], errors_here)
    return (errors_here, latent_grad)


def solution(mesh):
    placed = (P("layer", "feat"), P(), P(None, "feat", "layer"), P("feat", "layer"))
    on_line = mesh.shape["feat"] == 4 and mesh.shape["layer"] == 8
    return jax.shard_map(
        chain_local if on_line else local,
        mesh=mesh,
        in_specs=placed,
        out_specs=(P("feat", "layer"), P("layer", "feat")),
        check_vma=False,
    )
```
